32 devices in a mesh: groups: 2 (over x), tile: 16 (over z, y, core).
Axes of the slice: x: 2, y: 2, z: 4, core: 2. Of those that a mesh axis runs over, the one named last changes fastest.
Arguments:
- video_latent: bfloat16 [96, 160, 384], P(('groups', 'tile')), parts along dimension 0, may hold values from -6 to 6
- conv_cache: bfloat16 [96, 160, 384], P(('groups', 'tile')), parts along dimension 0, may hold values from -6 to 6
- norm_gain: float32 [384], replicated, may hold values from 0.1 to 1.9
- conv_kernel: bfloat16 [3, 3, 3, 384, 384], replicated, may hold values from -0.0625 to 0.0625
- attend_gain: float32 [384], replicated, may hold values from 0.1 to 1.9
- w_query: bfloat16 [384, 384], replicated, may hold values from -2 to 6
- w_key: bfloat16 [384, 384], replicated, may hold values from -2 to 6
- w_value: bfloat16 [384, 384], replicated, may hold values from -0.3125 to 0.3125
- w_output: bfloat16 [384, 384], replicated, may hold values from -0.3125 to 0.3125
Outputs:
- result: bfloat16 [96, 160, 384], P(('groups', 'tile')), parts along dimension 0
The draws below stay inside these ranges and needn't reach their ends.
There are 2 independent parts, one for each index of `groups`. The reference program is written for one: setup_inputs(seed, part) draws one part's arguments, and reference() takes and returns one part's arrays. A program takes and returns all parts, laid end to end along the dimension named above; an argument that names none is the same for every part. Nothing has to cross between parts.
All inputs are finite; a program needn't handle non-finite values.
Results may differ from the reference program's by a relative error of at most 0.007.
Values may be sent and summed in bfloat16 or wider, within the bound.
A program may use at most 64 MiB of HBM per device.

```python
import jax
import jax.numpy as jnp
from jax import lax

C = 384
ROWS_DEV = 3
COLS = 160
CACHED = 2
ROW_TILES = 8
FRAMES = 2
ROWS = 24


def projection_draw(key, salt):
    matrix = jax.random.truncated_normal(jax.random.fold_in(key, salt), -4.0, 4.0, (C, C), jnp.float32) * (1.7 * float(C) ** (-0.5))
    return matrix.astype(jnp.bfloat16)


def draw_w_query(key, part):
    return projection_draw(key, 11)


def draw_w_key(key, part):
    return projection_draw(key, 12)


def level_of(rng, dims, shards, low, largest):
    level, own = 1.0, jax.random.fold_in(rng, 6)
    for position, shards_of in shards:
        draws = jnp.exp(jax.random.uniform(jax.random.fold_in(own, position), (shards_of,), jnp.float32, low / len(shards), largest / len(shards)))
        level = level * jnp.repeat(draws, dims[position] // shards_of).reshape([-1 if axis == position else 1 for axis in range(len(dims))])
    return level


def scatter_about(rng, shape, width, limit, shards=(), held_as=jnp.bfloat16):
    drawn = jax.random.normal(rng, shape, jnp.float32) * width
    if len(shards) > 0:
        drawn = level_of(rng, shape, shards, -0.22, 0.18) * drawn
    return jnp.clip(drawn, min=-limit, max=limit).astype(held_as)


def setup_inputs(seed: int = 0, part: int = 0) -> dict:
    key_list = jax.random.split(jax.random.key(seed), 10)
    own_keys = jax.random.split(jax.random.fold_in(key_list[9], part), 10)
    video_latent = scatter_about(own_keys[0], (FRAMES * ROWS, COLS, C), 1.0, 6.0, ((0, 16),))
    conv_cache = scatter_about(own_keys[1], (FRAMES * ROWS, COLS, C), 1.0, 6.0, ((0, 16),))
    norm_gain = jnp.clip(1.0 + 0.18 * jax.random.normal(key_list[2], (C,), jnp.float32), 0.1, 1.9)
    conv_kernel = scatter_about(key_list[3], (3, 3, 3, C, C), (27 * C) ** -0.5, 0.0625)
    attend_gain = jnp.clip(1.0 + 0.18 * jax.random.normal(key_list[4], (C,), jnp.float32), 0.1, 1.9)
    w_query = draw_w_query(jax.random.fold_in(key_list[9], 71), part)
    w_key = draw_w_key(jax.random.fold_in(key_list[9], 71), part)
    w_value = scatter_about(key_list[7], (C, C), C ** -0.5, 0.3125)
    w_output = scatter_about(key_list[8], (C, C), C ** -0.5, 0.3125)
    return {"video_latent": video_latent, "conv_cache": conv_cache, "norm_gain": norm_gain, "conv_kernel": conv_kernel, "attend_gain": attend_gain, "w_query": w_query, "w_key": w_key, "w_value": w_value, "w_output": w_output}


def rms_scale(inputs, scale_gain):
    floats = inputs.astype(jnp.float32)
    return floats * lax.rsqrt(lax.optimization_barrier(jnp.mean(floats * floats, axis=-1, keepdims=True)) + 1e-06) * scale_gain

def causal_conv(inputs, kernel):
    depth_in, rows_all, cols_all, channels = inputs.shape
    frames_out = depth_in - 2
    padded = jnp.pad(inputs, ((0, 0), (1, 1), (1, 1), (0, 0)))
    summed = jnp.zeros((frames_out * rows_all * cols_all, channels), jnp.float32)
    for time_tap in range(3):
        for row_tap in range(3):
            for col_tap in range(3):
                window = padded[time_tap:time_tap + frames_out, row_tap:row_tap + rows_all, col_tap:col_tap + cols_all]
                summed = summed + jnp.dot(window.reshape(-1, channels), kernel[time_tap, row_tap, col_tap], preferred_element_type=jnp.float32)
    return summed.reshape(frames_out, rows_all, cols_all, channels)

def to_frames(blocks):
    return blocks.reshape(ROW_TILES, FRAMES, ROWS_DEV, COLS, C).transpose(1, 0, 2, 3, 4).reshape(FRAMES, ROWS, COLS, C)

def reference(video_latent, conv_cache, norm_gain, conv_kernel, attend_gain, w_query, w_key, w_value, w_output):
    latent = to_frames(video_latent)
    moved_cache = jnp.roll(conv_cache.reshape(ROW_TILES, FRAMES * ROWS_DEV, COLS, C), 1, axis=0)
    earlier = to_frames(moved_cache)[FRAMES - CACHED:]
    activated = jax.nn.silu(rms_scale(latent, norm_gain)).astype(jnp.bfloat16)
    stacked = jnp.concatenate([earlier, activated], axis=0)
    residual = (latent.astype(jnp.float32) + causal_conv(stacked, conv_kernel)).astype(jnp.bfloat16)
    normed = rms_scale(residual, attend_gain).astype(jnp.bfloat16)
    flat_rows = normed.reshape(-1, C)

    def project(weight):
        return jnp.dot(flat_rows, weight, preferred_element_type=jnp.float32).astype(jnp.bfloat16).reshape(FRAMES, ROWS, COLS, C)
    queries = project(w_query)
    keys_all = project(w_key)
    values_all = project(w_value)
    score_scale = float(C) ** (-0.5)

    def one_frame(frame_data):
        frame_queries, frame_keys, frame_values = frame_data
        frame_keys = frame_keys.reshape(-1, C)
        frame_values = frame_values.reshape(-1, C)

        def one_row(row_queries):
            scores = jnp.dot(row_queries, frame_keys.T, preferred_element_type=jnp.float32) * score_scale
            highest = lax.optimization_barrier(jnp.max(scores, axis=-1, keepdims=True))
            weights = jnp.exp(scores - highest)
            weight_sum = lax.optimization_barrier(jnp.sum(weights, axis=-1, keepdims=True))
            numerator = jnp.dot(weights.astype(jnp.bfloat16), frame_values, preferred_element_type=jnp.float32)
            return (numerator / weight_sum).astype(jnp.bfloat16)
        return lax.map(one_row, frame_queries)
    attended = lax.map(one_frame, (queries, keys_all, values_all))
    output_term = jnp.dot(attended.reshape(-1, C), w_output, preferred_element_type=jnp.float32).reshape(FRAMES, ROWS, COLS, C)
    final = (residual.astype(jnp.float32) + output_term).astype(jnp.bfloat16)
    final = final.reshape(FRAMES, ROW_TILES, ROWS_DEV, COLS, C).transpose(1, 0, 2, 3, 4)
    return final.reshape(FRAMES * ROWS, COLS, C)
```

```python
import functools

import jax
import jax.numpy as jnp
from jax import lax
from jax.experimental import pallas as pl
from jax.experimental.pallas import tpu as pltpu
from jax.sharding import PartitionSpec as P


def from_behind(value, axis, steps):
    count = lax.axis_size(axis)
    pairs = [(source, (source + steps) % count) for source in range(count)]
    return lax.ppermute(value, axis, pairs)


def passed_along(block, axis, distance):
    devices = range(lax.axis_size(axis))
    route = [(i - distance, i) for i in devices if i - distance in devices]
    return lax.ppermute(block, axis, route)


def rms_scale(inputs, scale_gain):
    floats = inputs.astype(jnp.float32)
    return (
        floats * lax.rsqrt(jnp.mean(floats * floats, axis=-1, keepdims=True) + 1e-06) * scale_gain
    )


def dot32(a, b):
    return jnp.dot(a, b, preferred_element_type=jnp.float32)


def ring_tile(place, row_tiles):
    half = row_tiles // 2
    return jnp.where(place < half, 2 * place, 2 * (row_tiles - 1 - place) + 1)


def attend_kernel(
    frames,
    row_tiles,
    pieces,
    normed_ref,
    residual_ref,
    wq_ref,
    wk_ref,
    wv_ref,
    wo_ref,
    out_ref,
    held,
    queries,
    highest,
    total,
    acc,
    send_sem,
    recv_sem,
):
    positions, channels = normed_ref.shape
    half = row_tiles // 2
    piece = positions // pieces
    scale = float(channels) ** (-0.5)
    me = lax.axis_index("tile")
    frame = lax.rem(me, frames)
    tile = lax.div(me, frames)
    place = jnp.where(
        lax.rem(tile, 2) == 0, lax.div(tile, 2), row_tiles - 1 - lax.div(tile, 2)
    )
    right = ring_tile(lax.rem(place + 1, row_tiles), row_tiles) * frames + frame
    left = ring_tile(lax.rem(place + row_tiles - 1, row_tiles), row_tiles) * frames + frame

    barrier = pltpu.get_barrier_semaphore()
    for neighbour in (left, right):
        pl.semaphore_signal(
            barrier, inc=1, device_id={"tile": neighbour}, device_id_type=pl.DeviceIdType.MESH
        )
    held[0] = normed_ref[...]
    pl.semaphore_wait(barrier, 2)

    def copy(way, step, part):
        if way == 0:
            source, target, peer = step - 1, step, right
        else:
            source, target, peer = (
                lax.rem(row_tiles - step + 1, row_tiles),
                row_tiles - step,
                left,
            )
        rows = pl.ds(pl.multiple_of(part * piece, piece), piece)
        return pltpu.make_async_remote_copy(
            src_ref=held.at[source, rows],
            dst_ref=held.at[target, rows],
            send_sem=send_sem.at[way, step, part],
            recv_sem=recv_sem.at[way, step, part],
            device_id={"tile": peer},
            device_id_type=pl.DeviceIdType.MESH,
        )

    def runs(way, step, part):
        last = (part < pieces // 2) if way == 0 else (part >= pieces // 2)
        return jnp.logical_or(step < half, jnp.logical_and(step == half, last))

    for part in range(pieces):
        for way in range(2):
            copy(way, 1, part).start()

    queries[...] = dot32(normed_ref[...], wq_ref[...]).astype(jnp.bfloat16)
    highest[...] = jnp.full(highest.shape, -1e30, jnp.float32)
    total[...] = jnp.zeros(total.shape, jnp.float32)
    acc[...] = jnp.zeros(acc.shape, jnp.float32)

    def absorb(slot, part):
        rows = pl.ds(pl.multiple_of(part * piece, piece), piece)
        block = held[slot, rows]
        keys = dot32(block, wk_ref[...]).astype(jnp.bfloat16)
        values = dot32(block, wv_ref[...]).astype(jnp.bfloat16)
        scores = (
            lax.dot_general(
                queries[...], keys, (((1,), (1,)), ((), ())), preferred_element_type=jnp.float32
            )
            * scale
        )
        before = highest[...]
        now = jnp.maximum(before, jnp.max(scores, axis=-1, keepdims=True))
        rescale = jnp.exp(before - now)
        weights = jnp.exp(scores - now)
        highest[...] = now
        total[...] = total[...] * rescale + jnp.sum(weights, axis=-1, keepdims=True)
        acc[...] = acc[...] * rescale + dot32(weights.astype(jnp.bfloat16), values)

    def own(part, carry):
        absorb(0, part)
        return carry

    lax.fori_loop(0, pieces, own, 0)

    def visit(index, carry):
        step = lax.div(index, pieces) + 1
        part = lax.rem(index, pieces)
        for way in range(2):

            @pl.when(runs(way, step, part))
            def _(way=way):
                copy(way, step, part).wait_recv()

            @pl.when(runs(way, step + 1, part))
            def _(way=way):
                copy(way, step + 1, part).start()

        def one(way, carry):
            absorb(jnp.where(way == 0, step, row_tiles - step), part)
            return carry

        lax.fori_loop(0, jnp.where(step == half, 1, 2), one, 0)
        return carry

    lax.fori_loop(0, half * pieces, visit, 0)

    attended = (acc[...] / total[...]).astype(jnp.bfloat16)
    out_ref[...] = (
        residual_ref[...].astype(jnp.float32) + dot32(attended, wo_ref[...])
    ).astype(jnp.bfloat16)

    def finish(index, carry):
        step = lax.div(index, pieces) + 1
        part = lax.rem(index, pieces)
        for way in range(2):

            @pl.when(runs(way, step, part))
            def _(way=way):
                copy(way, step, part).wait_send()

        return carry

    lax.fori_loop(0, half * pieces, finish, 0)


def attend(normed, residual, weights, frames, row_tiles, pieces=2):
    positions, channels = normed.shape
    half = row_tiles // 2
    return pl.pallas_call(
        functools.partial(attend_kernel, frames, row_tiles, pieces),
        out_shape=jax.ShapeDtypeStruct((positions, channels), jnp.bfloat16),
        in_specs=[pl.BlockSpec(memory_space=pltpu.VMEM)] * 6,
        out_specs=pl.BlockSpec(memory_space=pltpu.VMEM),
        scratch_shapes=[
            pltpu.VMEM((row_tiles, positions, channels), jnp.bfloat16),
            pltpu.VMEM((positions, channels), jnp.bfloat16),
            pltpu.VMEM((positions, 1), jnp.float32),
            pltpu.VMEM((positions, 1), jnp.float32),
            pltpu.VMEM((positions, channels), jnp.float32),
            pltpu.SemaphoreType.DMA((2, half + 1, pieces)),
            pltpu.SemaphoreType.DMA((2, half + 1, pieces)),
        ],
        compiler_params=pltpu.CompilerParams(
            collective_id=0, has_side_effects=True, vmem_limit_bytes=40 * 2**20
        ),
    )(normed, residual, *weights)


def body(
    video_latent, conv_cache, norm_gain, conv_kernel, attend_gain, w_query, w_key, w_value, w_output
):
    rows_local, cols_all, channels = video_latent.shape
    tiles = lax.axis_size("tile")
    row_tiles = min(16, tiles // 2)
    frames = tiles // row_tiles
    position = lax.axis_index("tile")
    time_group = position % frames
    activated = jax.nn.silu(rms_scale(video_latent, norm_gain)).astype(jnp.bfloat16)
    frame_pair = jnp.stack([activated, conv_cache])
    before_one = from_behind(frame_pair, "tile", 1)
    before_two = from_behind(before_one, "tile", 1)
    frame_one = jnp.where(time_group >= 1, before_one[0], before_one[1])
    frame_two = jnp.where(time_group >= 2, before_two[0], before_two[1])
    stacked = jnp.stack([frame_two, frame_one, frame_pair[0]])
    rim_above = passed_along(stacked[:, -1:], "tile", frames)
    rim_below = passed_along(stacked[:, :1], "tile", -frames)
    stacked = jnp.concatenate([rim_above, stacked, rim_below], axis=1)
    padded = jnp.pad(stacked, ((0, 0), (0, 0), (1, 1), (0, 0)))
    summed = jnp.zeros((rows_local * cols_all, channels), jnp.float32)
    for time_tap in range(3):
        for row_tap in range(3):
            for col_tap in range(3):
                window = padded[
                    time_tap, row_tap : row_tap + rows_local, col_tap : col_tap + cols_all
                ]
                summed = summed + dot32(
                    window.reshape(-1, channels), conv_kernel[time_tap, row_tap, col_tap]
                )
    residual = (video_latent.astype(jnp.float32) + summed.reshape(video_latent.shape)).astype(
        jnp.bfloat16
    )
    normed = rms_scale(residual, attend_gain).astype(jnp.bfloat16)
    result = attend(
        normed.reshape(-1, channels),
        residual.reshape(-1, channels),
        (w_query, w_key, w_value, w_output),
        frames,
        row_tiles,
    )
    return result.reshape(video_latent.shape)


def solution(mesh):
    placed = (
        P(("groups", "tile"), None, None),
        P(("groups", "tile"), None, None),
        P(),
        P(),
        P(),
        P(),
        P(),
        P(),
        P(),
    )
    return jax.shard_map(
        body,
        mesh=mesh,
        in_specs=placed,
        out_specs=P(("groups", "tile"), None, None),
        check_vma=False,
    )
```

```python
import functools

import jax
import jax.numpy as jnp
from jax import lax
from jax.experimental import pallas as pl
from jax.experimental.pallas import tpu as pltpu
from jax.sharding import PartitionSpec as P


def from_behind(value, axis, steps):
    count = lax.axis_size(axis)
    pairs = [(source, (source + steps) % count) for source in range(count)]
    return lax.ppermute(value, axis, pairs)


def passed_along(block, axis, distance):
    devices = range(lax.axis_size(axis))
    route = [(i - distance, i) for i in devices if i - distance in devices]
    return lax.ppermute(block, axis, route)


def rms_scale(inputs, scale_gain):
    floats = inputs.astype(jnp.float32)
    return (
        floats * lax.rsqrt(jnp.mean(floats * floats, axis=-1, keepdims=True) + 1e-06) * scale_gain
    )


def dot32(a, b):
    return jnp.dot(a, b, preferred_element_type=jnp.float32)


def ring_tile(place, row_tiles):
    half = row_tiles // 2
    return jnp.where(place < half, 2 * place, 2 * (row_tiles - 1 - place) + 1)


MESH = pl.DeviceIdType.MESH


def place_of(tile, row_tiles):
    return jnp.where(lax.rem(tile, 2) == 0, lax.div(tile, 2), row_tiles - 1 - lax.div(tile, 2))


def ring_neighbours(tile, row_tiles):
    place = place_of(tile, row_tiles)
    right = ring_tile(lax.rem(place + 1, row_tiles), row_tiles)
    left = ring_tile(lax.rem(place + row_tiles - 1, row_tiles), row_tiles)
    return left, right


def attend_ring(
    row_tiles,
    pieces,
    left,
    right,
    residual_ref,
    wq_ref,
    wk_ref,
    wv_ref,
    wo_ref,
    out_ref,
    held,
    queries,
    highest,
    total,
    acc,
    send_sem,
    recv_sem,
):
    positions, channels = residual_ref.shape
    half = row_tiles // 2
    piece = positions // pieces
    scale = float(channels) ** (-0.5)

    def copy(way, step, part):
        if way == 0:
            source, target, peer = step - 1, step, right
        else:
            source, target, peer = (
                lax.rem(row_tiles - step + 1, row_tiles),
                row_tiles - step,
                left,
            )
        rows = pl.ds(pl.multiple_of(part * piece, piece), piece)
        return pltpu.make_async_remote_copy(
            src_ref=held.at[source, rows],
            dst_ref=held.at[target, rows],
            send_sem=send_sem.at[way, step, part],
            recv_sem=recv_sem.at[way, step, part],
            device_id={"tile": peer},
            device_id_type=pl.DeviceIdType.MESH,
        )

    def runs(way, step, part):
        last = (part < pieces // 2) if way == 0 else (part >= pieces // 2)
        return jnp.logical_or(step < half, jnp.logical_and(step == half, last))

    for part in range(pieces):
        for way in range(2):
            copy(way, 1, part).start()

    queries[...] = dot32(held[0], wq_ref[...]).astype(jnp.bfloat16)
    highest[...] = jnp.full(highest.shape, -1e30, jnp.float32)
    total[...] = jnp.zeros(total.shape, jnp.float32)
    acc[...] = jnp.zeros(acc.shape, jnp.float32)

    def absorb(slot, part):
        rows = pl.ds(pl.multiple_of(part * piece, piece), piece)
        block = held[slot, rows]
        keys = dot32(block, wk_ref[...]).astype(jnp.bfloat16)
        values = dot32(block, wv_ref[...]).astype(jnp.bfloat16)
        scores = (
            lax.dot_general(
                queries[...], keys, (((1,), (1,)), ((), ())), preferred_element_type=jnp.float32
            )
            * scale
        )
        before = highest[...]
        now = jnp.maximum(before, jnp.max(scores, axis=-1, keepdims=True))
        rescale = jnp.exp(before - now)
        weights = jnp.exp(scores - now)
        highest[...] = now
        total[...] = total[...] * rescale + jnp.sum(weights, axis=-1, keepdims=True)
        acc[...] = acc[...] * rescale + dot32(weights.astype(jnp.bfloat16), values)

    def own(part, carry):
        absorb(0, part)
        return carry

    lax.fori_loop(0, pieces, own, 0)

    def visit(index, carry):
        step = lax.div(index, pieces) + 1
        part = lax.rem(index, pieces)
        for way in range(2):

            @pl.when(runs(way, step, part))
            def _(way=way):
                copy(way, step, part).wait_recv()

            @pl.when(runs(way, step + 1, part))
            def _(way=way):
                copy(way, step + 1, part).start()

        def one(way, carry):
            absorb(jnp.where(way == 0, step, row_tiles - step), part)
            return carry

        lax.fori_loop(0, jnp.where(step == half, 1, 2), one, 0)
        return carry

    lax.fori_loop(0, half * pieces, visit, 0)

    attended = (acc[...] / total[...]).astype(jnp.bfloat16)
    out_ref[...] = (
        residual_ref[...].astype(jnp.float32) + dot32(attended, wo_ref[...])
    ).astype(jnp.bfloat16)

    def finish(index, carry):
        step = lax.div(index, pieces) + 1
        part = lax.rem(index, pieces)
        for way in range(2):

            @pl.when(runs(way, step, part))
            def _(way=way):
                copy(way, step, part).wait_send()

        return carry

    lax.fori_loop(0, half * pieces, finish, 0)


def attend_kernel(
    frames, row_tiles, pieces, normed_ref, residual_ref, wq, wk, wv, wo, out_ref, held, *scratch
):
    me = lax.axis_index("tile")
    frame = lax.rem(me, frames)
    left, right = ring_neighbours(lax.div(me, frames), row_tiles)
    left, right = left * frames + frame, right * frames + frame
    barrier = pltpu.get_barrier_semaphore()
    for neighbour in (left, right):
        pl.semaphore_signal(barrier, inc=1, device_id={"tile": neighbour}, device_id_type=MESH)
    held[0] = normed_ref[...]
    pl.semaphore_wait(barrier, 2)
    attend_ring(
        row_tiles, pieces, left, right, residual_ref, wq, wk, wv, wo, out_ref, held, *scratch
    )


def ring_scratch(row_tiles, pieces, positions, channels):
    half = row_tiles // 2
    return [
        pltpu.VMEM((row_tiles, positions, channels), jnp.bfloat16),
        pltpu.VMEM((positions, channels), jnp.bfloat16),
        pltpu.VMEM((positions, 1), jnp.float32),
        pltpu.VMEM((positions, 1), jnp.float32),
        pltpu.VMEM((positions, channels), jnp.float32),
        pltpu.SemaphoreType.DMA((2, half + 1, pieces)),
        pltpu.SemaphoreType.DMA((2, half + 1, pieces)),
    ]


def attend(normed, residual, weights, frames, row_tiles, pieces=2):
    positions, channels = normed.shape
    return pl.pallas_call(
        functools.partial(attend_kernel, frames, row_tiles, pieces),
        out_shape=jax.ShapeDtypeStruct((positions, channels), jnp.bfloat16),
        in_specs=[pl.BlockSpec(memory_space=pltpu.VMEM)] * 6,
        out_specs=pl.BlockSpec(memory_space=pltpu.VMEM),
        scratch_shapes=ring_scratch(row_tiles, pieces, positions, channels),
        compiler_params=pltpu.CompilerParams(
            collective_id=0, has_side_effects=True, vmem_limit_bytes=40 * 2**20
        ),
    )(normed, residual, *weights)


def block_kernel(
    row_tiles,
    pieces,
    latent_ref,
    cache_ref,
    gain_ref,
    kernel_ref,
    gain2_ref,
    wq,
    wk,
    wv,
    wo,
    out_ref,
    held,
    queries,
    highest,
    total,
    acc,
    send_sem,
    recv_sem,
    stack,
    taps,
    conv,
    residual,
    tap_sem,
    out_sem,
    row_sem,
):
    rows, cols, channels = latent_ref.shape
    positions = rows * cols
    me = lax.axis_index("tile")
    frame = lax.rem(me, 2)
    tile = lax.div(me, 2)
    other = me + 1 - 2 * frame
    ring_left, ring_right = ring_neighbours(tile, row_tiles)

    def wrapped(by):
        return lax.rem(tile + by + row_tiles, row_tiles) * 2 + frame

    barrier = pltpu.get_barrier_semaphore()
    for partner in (wrapped(1), wrapped(-1), wrapped(2), wrapped(-2), other):
        pl.semaphore_signal(barrier, inc=1, device_id={"tile": partner}, device_id_type=MESH)

    def tap_copy(t, i, j):
        return pltpu.make_async_copy(
            kernel_ref.at[t, i, j],
            taps.at[t, i * channels : (i + 1) * channels, j * channels : (j + 1) * channels],
            tap_sem.at[t, i, j],
        )

    every = [(i, j) for i in range(3) for j in range(3)]
    for t in (2, 0, 1):
        for i, j in every:
            tap_copy(t, i, j).start()

    first, last = tile == 0, tile == row_tiles - 1
    owned = lax.rem(tile + 1, row_tiles)

    def send(source, slot, row, number, device):
        return pltpu.make_async_remote_copy(
            src_ref=source,
            dst_ref=stack.at[slot, row],
            send_sem=out_sem.at[number],
            recv_sem=row_sem.at[slot, row],
            device_id={"tile": device},
            device_id_type=MESH,
        )

    cache_rows = [send(cache_ref.at[j], 0, 1 + j, j, wrapped(1)) for j in range(rows)]
    cache_rim = send(cache_ref.at[rows - 1], 0, 0, rows, wrapped(2))
    rim_down = send(stack.at[2, rows], 2, 0, rows + 1, wrapped(1))
    rim_up = send(stack.at[2, 1], 2, rows + 1, rows + 2, wrapped(-1))
    shared = 2 - 2 * frame
    onward = [send(stack.at[shared, j], 1, j, rows + 3 + j, other) for j in range(rows + 2)]

    pl.semaphore_wait(barrier, 5)
    for copy in cache_rows:
        copy.start()

    @pl.when(owned + 1 < row_tiles)
    def _():
        cache_rim.start()

    floats = latent_ref[...].astype(jnp.float32)
    scaled = (
        floats
        * lax.rsqrt(jnp.mean(floats * floats, axis=-1, keepdims=True) + 1e-06)
        * gain_ref[...]
    )
    stack[2, 1 : rows + 1] = (scaled / (1.0 + jnp.exp(-scaled))).astype(jnp.bfloat16)

    @pl.when(jnp.logical_not(last))
    def _():
        rim_down.start()

    @pl.when(jnp.logical_not(first))
    def _():
        rim_up.start()

    @pl.when(frame == 0)
    def _():
        for j in range(1, rows + 1):
            onward[j].start()

    nothing = jnp.zeros((cols, channels), jnp.bfloat16)

    @pl.when(first)
    def _():
        stack[0, 0] = nothing
        stack[2, 0] = nothing

    @pl.when(last)
    def _():
        stack[0, rows + 1] = nothing
        stack[2, rows + 1] = nothing

    @pl.when(jnp.logical_not(last))
    def _():
        stack[0, rows + 1] = cache_ref[0]

    def arrived(slot, row):
        send(stack.at[slot, row], slot, row, 0, other).wait_recv()

    def cached_in():
        for j in range(1, rows + 1):
            arrived(0, j)
            yield j

        @pl.when(jnp.logical_not(first))
        def _():
            arrived(0, 0)

        yield 0

    def step(turn, carry):
        slot = jnp.where(turn == 0, 2, jnp.where(turn == 1, frame, 1 - frame))

        @pl.when(turn == 0)
        def _():
            @pl.when(jnp.logical_not(first))
            def _():
                arrived(2, 0)

            @pl.when(jnp.logical_not(last))
            def _():
                arrived(2, rows + 1)

            @pl.when(frame == 0)
            def _():
                onward[0].start()
                onward[rows + 1].start()

            @pl.when(frame == 1)
            def _():
                onward[rows + 1].start()

        @pl.when(jnp.logical_and(turn > 0, slot == 1))
        def _():
            for j in range(rows + 2):
                arrived(1, j)

        @pl.when(jnp.logical_and(turn > 0, jnp.logical_and(slot == 0, frame == 0)))
        def _():
            for j in cached_in():
                pass

        @pl.when(jnp.logical_and(turn > 0, jnp.logical_and(slot == 0, frame == 1)))
        def _():
            for j in cached_in():
                onward[j].start()

        for i, j in every:
            pltpu.make_async_copy(
                kernel_ref.at[slot, i, j],
                taps.at[
                    slot, i * channels : (i + 1) * channels, j * channels : (j + 1) * channels
                ],
                tap_sem.at[slot, i, j],
            ).wait()

        window = jnp.concatenate(
            [stack[slot, i : i + rows].reshape(positions, channels) for i in range(3)], axis=-1
        )
        product = dot32(window, taps[slot])

        @pl.when(turn == 0)
        def _():
            conv[...] = product

        @pl.when(turn > 0)
        def _():
            conv[...] += product

        return carry

    lax.fori_loop(0, 3, step, 0)

    column = lax.rem(lax.broadcasted_iota(jnp.int32, (positions, 1), 0), cols)
    before = pltpu.roll(conv[:, :channels], 1, 0)
    after = pltpu.roll(conv[:, 2 * channels :], positions - 1, 0)
    summed = (
        jnp.where(column == 0, 0.0, before)
        + conv[:, channels : 2 * channels]
        + jnp.where(column == cols - 1, 0.0, after)
    )
    rounded = (
        latent_ref[...].reshape(positions, channels).astype(jnp.float32) + summed
    ).astype(jnp.bfloat16)
    residual[...] = rounded
    wide = rounded.astype(jnp.float32)
    held[0] = (
        wide * lax.rsqrt(jnp.mean(wide * wide, axis=-1, keepdims=True) + 1e-06) * gain2_ref[...]
    ).astype(jnp.bfloat16)

    attend_ring(
        row_tiles,
        pieces,
        ring_left * 2 + frame,
        ring_right * 2 + frame,
        residual,
        wq,
        wk,
        wv,
        wo,
        out_ref,
        held,
        queries,
        highest,
        total,
        acc,
        send_sem,
        recv_sem,
    )

    for copy in cache_rows + onward:
        copy.wait_send()

    @pl.when(owned + 1 < row_tiles)
    def _():
        cache_rim.wait_send()

    @pl.when(jnp.logical_not(last))
    def _():
        rim_down.wait_send()

    @pl.when(jnp.logical_not(first))
    def _():
        rim_up.wait_send()


def whole_block(latent, cache, norm_gain, conv_kernel, attend_gain, weights, row_tiles, pieces=2):
    rows, cols, channels = latent.shape
    positions = rows * cols
    held_in_vmem = pl.BlockSpec(memory_space=pltpu.VMEM)
    return pl.pallas_call(
        functools.partial(block_kernel, row_tiles, pieces),
        out_shape=jax.ShapeDtypeStruct((positions, channels), jnp.bfloat16),
        in_specs=[held_in_vmem] * 3 + [pl.BlockSpec(memory_space=pl.ANY)] + [held_in_vmem] * 5,
        out_specs=held_in_vmem,
        scratch_shapes=ring_scratch(row_tiles, pieces, positions, channels)
        + [
            pltpu.VMEM((3, rows + 2, cols, channels), jnp.bfloat16),
            pltpu.VMEM((3, 3 * channels, 3 * channels), jnp.bfloat16),
            pltpu.VMEM((positions, 3 * channels), jnp.float32),
            pltpu.VMEM((positions, channels), jnp.bfloat16),
            pltpu.SemaphoreType.DMA((3, 3, 3)),
            pltpu.SemaphoreType.DMA((2 * rows + 5,)),
            pltpu.SemaphoreType.DMA((3, rows + 2)),
        ],
        compiler_params=pltpu.CompilerParams(
            collective_id=0, has_side_effects=True, vmem_limit_bytes=56 * 2**20
        ),
    )(
        latent,
        cache,
        norm_gain.reshape(1, channels),
        conv_kernel,
        attend_gain.reshape(1, channels),
        *weights,
    )


def body(
    video_latent, conv_cache, norm_gain, conv_kernel, attend_gain, w_query, w_key, w_value, w_output
):
    rows_local, cols_all, channels = video_latent.shape
    tiles = lax.axis_size("tile")
    row_tiles = min(16, tiles // 2)
    frames = tiles // row_tiles
    if frames == 2 and row_tiles > 4:
        result = whole_block(
            video_latent,
            conv_cache,
            norm_gain,
            conv_kernel,
            attend_gain,
            (w_query, w_key, w_value, w_output),
            row_tiles,
        )
        return result.reshape(video_latent.shape)
    position = lax.axis_index("tile")
    time_group = position % frames
    activated = jax.nn.silu(rms_scale(video_latent, norm_gain)).astype(jnp.bfloat16)
    frame_pair = jnp.stack([activated, conv_cache])
    before_one = from_behind(frame_pair, "tile", 1)
    before_two = from_behind(before_one, "tile", 1)
    frame_one = jnp.where(time_group >= 1, before_one[0], before_one[1])
    frame_two = jnp.where(time_group >= 2, before_two[0], before_two[1])
    stacked = jnp.stack([frame_two, frame_one, frame_pair[0]])
    rim_above = passed_along(stacked[:, -1:], "tile", frames)
    rim_below = passed_along(stacked[:, :1], "tile", -frames)
    stacked = jnp.concatenate([rim_above, stacked, rim_below], axis=1)
    padded = jnp.pad(stacked, ((0, 0), (0, 0), (1, 1), (0, 0)))
    summed = jnp.zeros((rows_local * cols_all, channels), jnp.float32)
    for time_tap in range(3):
        for row_tap in range(3):
            for col_tap in range(3):
                window = padded[
                    time_tap, row_tap : row_tap + rows_local, col_tap : col_tap + cols_all
                ]
                summed = summed + dot32(
                    window.reshape(-1, channels), conv_kernel[time_tap, row_tap, col_tap]
                )
    residual = (video_latent.astype(jnp.float32) + summed.reshape(video_latent.shape)).astype(
        jnp.bfloat16
    )
    normed = rms_scale(residual, attend_gain).astype(jnp.bfloat16)
    result = attend(
        normed.reshape(-1, channels),
        residual.reshape(-1, channels),
        (w_query, w_key, w_value, w_output),
        frames,
        row_tiles,
    )
    return result.reshape(video_latent.shape)


def solution(mesh):
    placed = (
        P(("groups", "tile"), None, None),
        P(("groups", "tile"), None, None),
        P(),
        P(),
        P(),
        P(),
        P(),
        P(),
        P(),
    )
    return jax.shard_map(
        body,
        mesh=mesh,
        in_specs=placed,
        out_specs=P(("groups", "tile"), None, None),
        check_vma=False,
    )
```

```python
import functools

import jax
import jax.numpy as jnp
from jax import lax
from jax.experimental import pallas as pl
from jax.experimental.pallas import tpu as pltpu
from jax.sharding import PartitionSpec as P


def from_behind(value, axis, steps):
    count = lax.axis_size(axis)
    pairs = [(source, (source + steps) % count) for source in range(count)]
    return lax.ppermute(value, axis, pairs)


def passed_along(block, axis, distance):
    devices = range(lax.axis_size(axis))
    route = [(i - distance, i) for i in devices if i - distance in devices]
    return lax.ppermute(block, axis, route)


def rms_scale(inputs, scale_gain):
    floats = inputs.astype(jnp.float32)
    return (
        floats * lax.rsqrt(jnp.mean(floats * floats, axis=-1, keepdims=True) + 1e-06) * scale_gain
    )


def dot32(a, b):
    return jnp.dot(a, b, preferred_element_type=jnp.float32)


def ring_tile(place, row_tiles):
    half = row_tiles // 2
    return jnp.where(place < half, 2 * place, 2 * (row_tiles - 1 - place) + 1)


MESH = pl.DeviceIdType.MESH


def place_of(tile, row_tiles):
    return jnp.where(lax.rem(tile, 2) == 0, lax.div(tile, 2), row_tiles - 1 - lax.div(tile, 2))


def ring_neighbours(tile, row_tiles):
    place = place_of(tile, row_tiles)
    right = ring_tile(lax.rem(place + 1, row_tiles), row_tiles)
    left = ring_tile(lax.rem(place + row_tiles - 1, row_tiles), row_tiles)
    return left, right


def attend_ring(
    row_tiles,
    pieces,
    left,
    right,
    residual_ref,
    wq_ref,
    wk_ref,
    wv_ref,
    wo_ref,
    out_ref,
    held,
    queries,
    highest,
    total,
    acc,
    send_sem,
    recv_sem,
):
    positions, channels = residual_ref.shape
    half = row_tiles // 2
    piece = positions // pieces
    scale = float(channels) ** (-0.5)

    def copy(way, step, part):
        if way == 0:
            source, target, peer = step - 1, step, right
        else:
            source, target, peer = (
                lax.rem(row_tiles - step + 1, row_tiles),
                row_tiles - step,
                left,
            )
        rows = pl.ds(pl.multiple_of(part * piece, piece), piece)
        return pltpu.make_async_remote_copy(
            src_ref=held.at[source, rows],
            dst_ref=held.at[target, rows],
            send_sem=send_sem.at[way, step, part],
            recv_sem=recv_sem.at[way, step, part],
            device_id={"tile": peer},
            device_id_type=pl.DeviceIdType.MESH,
        )

    def runs(way, step, part):
        last = (part < pieces // 2) if way == 0 else (part >= pieces // 2)
        return jnp.logical_or(step < half, jnp.logical_and(step == half, last))

    for part in range(pieces):
        for way in range(2):
            copy(way, 1, part).start()

    queries[...] = dot32(held[0], wq_ref[...]).astype(jnp.bfloat16)
    highest[...] = jnp.full(highest.shape, -1e30, jnp.float32)
    total[...] = jnp.zeros(total.shape, jnp.float32)
    acc[...] = jnp.zeros(acc.shape, jnp.float32)

    def absorb(slot, part):
        rows = pl.ds(pl.multiple_of(part * piece, piece), piece)
        block = held[slot, rows]
        keys = dot32(block, wk_ref[...]).astype(jnp.bfloat16)
        values = dot32(block, wv_ref[...]).astype(jnp.bfloat16)
        scores = (
            lax.dot_general(
                queries[...], keys, (((1,), (1,)), ((), ())), preferred_element_type=jnp.float32
            )
            * scale
        )
        before = highest[...]
        now = jnp.maximum(before, jnp.max(scores, axis=-1, keepdims=True))
        rescale = jnp.exp(before - now)
        weights = jnp.exp(scores - now)
        highest[...] = now
        total[...] = total[...] * rescale + jnp.sum(weights, axis=-1, keepdims=True)
        acc[...] = acc[...] * rescale + dot32(weights.astype(jnp.bfloat16), values)

    def own(part, carry):
        absorb(0, part)
        return carry

    lax.fori_loop(0, pieces, own, 0)

    def visit(index, carry):
        step = lax.div(index, pieces) + 1
        part = lax.rem(index, pieces)
        for way in range(2):

            @pl.when(runs(way, step, part))
            def _(way=way):
                copy(way, step, part).wait_recv()

            @pl.when(runs(way, step + 1, part))
            def _(way=way):
                copy(way, step + 1, part).start()

        def one(way, carry):
            absorb(jnp.where(way == 0, step, row_tiles - step), part)
            return carry

        lax.fori_loop(0, jnp.where(step == half, 1, 2), one, 0)
        return carry

    lax.fori_loop(0, half * pieces, visit, 0)

    attended = (acc[...] / total[...]).astype(jnp.bfloat16)
    out_ref[...] = (
        residual_ref[...].astype(jnp.float32) + dot32(attended, wo_ref[...])
    ).astype(jnp.bfloat16)

    def finish(index, carry):
        step = lax.div(index, pieces) + 1
        part = lax.rem(index, pieces)
        for way in range(2):

            @pl.when(runs(way, step, part))
            def _(way=way):
                copy(way, step, part).wait_send()

        return carry

    lax.fori_loop(0, half * pieces, finish, 0)


def attend_kernel(
    frames, row_tiles, pieces, normed_ref, residual_ref, wq, wk, wv, wo, out_ref, held, *scratch
):
    me = lax.axis_index("tile")
    frame = lax.rem(me, frames)
    left, right = ring_neighbours(lax.div(me, frames), row_tiles)
    left, right = left * frames + frame, right * frames + frame
    barrier = pltpu.get_barrier_semaphore()
    for neighbour in (left, right):
        pl.semaphore_signal(barrier, inc=1, device_id={"tile": neighbour}, device_id_type=MESH)
    held[0] = normed_ref[...]
    pl.semaphore_wait(barrier, 2)
    attend_ring(
        row_tiles, pieces, left, right, residual_ref, wq, wk, wv, wo, out_ref, held, *scratch
    )


def ring_scratch(row_tiles, pieces, positions, channels):
    half = row_tiles // 2
    return [
        pltpu.VMEM((row_tiles, positions, channels), jnp.bfloat16),
        pltpu.VMEM((positions, channels), jnp.bfloat16),
        pltpu.VMEM((positions, 1), jnp.float32),
        pltpu.VMEM((positions, 1), jnp.float32),
        pltpu.VMEM((positions, channels), jnp.float32),
        pltpu.SemaphoreType.DMA((2, half + 1, pieces)),
        pltpu.SemaphoreType.DMA((2, half + 1, pieces)),
    ]


def attend(normed, residual, weights, frames, row_tiles, pieces=2):
    positions, channels = normed.shape
    return pl.pallas_call(
        functools.partial(attend_kernel, frames, row_tiles, pieces),
        out_shape=jax.ShapeDtypeStruct((positions, channels), jnp.bfloat16),
        in_specs=[pl.BlockSpec(memory_space=pltpu.VMEM)] * 6,
        out_specs=pl.BlockSpec(memory_space=pltpu.VMEM),
        scratch_shapes=ring_scratch(row_tiles, pieces, positions, channels),
        compiler_params=pltpu.CompilerParams(
            collective_id=0, has_side_effects=True, vmem_limit_bytes=40 * 2**20
        ),
    )(normed, residual, *weights)


def block_kernel(
    row_tiles,
    pieces,
    latent_hbm,
    cache_ref,
    gain_hbm,
    kernel_ref,
    gain2_hbm,
    wq_hbm,
    wk_hbm,
    wv_hbm,
    wo_hbm,
    out_ref,
    held,
    queries,
    highest,
    total,
    acc,
    send_sem,
    recv_sem,
    stack,
    taps,
    conv,
    residual,
    wq,
    wk,
    wv,
    wo,
    latent_ref,
    gain_ref,
    gain2_ref,
    tap_sem,
    weight_sem,
    out_sem,
    row_sem,
):
    rows, cols, channels = latent_hbm.shape
    positions = rows * cols
    me = lax.axis_index("tile")
    frame = lax.rem(me, 2)
    tile = lax.div(me, 2)
    other = me + 1 - 2 * frame
    ring_left, ring_right = ring_neighbours(tile, row_tiles)

    def wrapped(by):
        return lax.rem(tile + by + row_tiles, row_tiles) * 2 + frame

    barrier = pltpu.get_barrier_semaphore()
    for partner in (wrapped(1), wrapped(-1), wrapped(2), wrapped(-2), other):
        pl.semaphore_signal(barrier, inc=1, device_id={"tile": partner}, device_id_type=MESH)

    early = [
        pltpu.make_async_copy(source, target, weight_sem.at[5 + number])
        for number, (source, target) in enumerate(
            ((latent_hbm, latent_ref), (gain_hbm, gain_ref), (gain2_hbm, gain2_ref))
        )
    ]
    for load in early:
        load.start()

    def tap_copy(t, i, j):
        return pltpu.make_async_copy(
            kernel_ref.at[t, i, j],
            taps.at[t, i * channels : (i + 1) * channels, j * channels : (j + 1) * channels],
            tap_sem.at[t, i, j],
        )

    every = [(i, j) for i in range(3) for j in range(3)]
    for t in (2, 0, 1):
        for i, j in every:
            tap_copy(t, i, j).start()
    loads = [
        pltpu.make_async_copy(source, target, weight_sem.at[number])
        for number, (source, target) in enumerate(
            ((wq_hbm, wq), (wk_hbm, wk), (wv_hbm, wv), (wo_hbm, wo))
        )
    ]
    for load in loads:
        load.start()

    first, last = tile == 0, tile == row_tiles - 1
    owned = lax.rem(tile + 1, row_tiles)

    def send(source, slot, row, number, device):
        return pltpu.make_async_remote_copy(
            src_ref=source,
            dst_ref=stack.at[slot, row],
            send_sem=out_sem.at[number],
            recv_sem=row_sem.at[slot, row],
            device_id={"tile": device},
            device_id_type=MESH,
        )

    cache_rows = [send(cache_ref.at[j], 0, 1 + j, j, wrapped(1)) for j in range(rows)]
    cache_rim = send(cache_ref.at[rows - 1], 0, 0, rows, wrapped(2))
    rim_down = send(stack.at[2, rows], 2, 0, rows + 1, wrapped(1))
    rim_up = send(stack.at[2, 1], 2, rows + 1, rows + 2, wrapped(-1))
    shared = 2 - 2 * frame
    onward = [send(stack.at[shared, j], 1, j, rows + 3 + j, other) for j in range(rows + 2)]

    own_rim = pltpu.make_async_copy(cache_ref.at[0], stack.at[0, rows + 1], weight_sem.at[4])
    pl.semaphore_wait(barrier, 5)
    cache_rows[0].start()

    @pl.when(owned + 1 < row_tiles)
    def _():
        cache_rim.start()

    for load in early:
        load.wait()
    floats = latent_ref[...].astype(jnp.float32)
    scaled = (
        floats
        * lax.rsqrt(jnp.mean(floats * floats, axis=-1, keepdims=True) + 1e-06)
        * gain_ref[...].reshape(1, 1, channels)
    )
    stack[2, 1 : rows + 1] = (scaled / (1.0 + jnp.exp(-scaled))).astype(jnp.bfloat16)

    @pl.when(jnp.logical_not(last))
    def _():
        rim_down.start()

    @pl.when(jnp.logical_not(first))
    def _():
        rim_up.start()

    @pl.when(frame == 0)
    def _():
        for j in range(1, rows + 1):
            onward[j].start()

    for copy in cache_rows[1:]:
        copy.start()

    nothing = jnp.zeros((cols, channels), jnp.bfloat16)

    @pl.when(first)
    def _():
        stack[0, 0] = nothing
        stack[2, 0] = nothing

    @pl.when(last)
    def _():
        stack[0, rows + 1] = nothing
        stack[2, rows + 1] = nothing

    @pl.when(jnp.logical_not(last))
    def _():
        own_rim.start()
        own_rim.wait()

    def arrived(slot, row):
        send(stack.at[slot, row], slot, row, 0, other).wait_recv()

    def cached_in():
        for j in range(1, rows + 1):
            arrived(0, j)
            yield j

        @pl.when(jnp.logical_not(first))
        def _():
            arrived(0, 0)

        yield 0

    def step(turn, carry):
        slot = jnp.where(turn == 0, 2, jnp.where(turn == 1, frame, 1 - frame))

        @pl.when(turn == 0)
        def _():
            @pl.when(jnp.logical_not(first))
            def _():
                arrived(2, 0)

            @pl.when(jnp.logical_not(last))
            def _():
                arrived(2, rows + 1)

            @pl.when(frame == 0)
            def _():
                onward[0].start()
                onward[rows + 1].start()

            @pl.when(frame == 1)
            def _():
                onward[rows + 1].start()

        @pl.when(jnp.logical_and(turn > 0, slot == 1))
        def _():
            for j in range(rows + 2):
                arrived(1, j)

        @pl.when(jnp.logical_and(turn > 0, jnp.logical_and(slot == 0, frame == 0)))
        def _():
            for j in cached_in():
                pass

        @pl.when(jnp.logical_and(turn > 0, jnp.logical_and(slot == 0, frame == 1)))
        def _():
            for j in cached_in():
                onward[j].start()

        for i, j in every:
            pltpu.make_async_copy(
                kernel_ref.at[slot, i, j],
                taps.at[
                    slot, i * channels : (i + 1) * channels, j * channels : (j + 1) * channels
                ],
                tap_sem.at[slot, i, j],
            ).wait()

        window = jnp.concatenate(
            [stack[slot, i : i + rows].reshape(positions, channels) for i in range(3)], axis=-1
        )
        product = dot32(window, taps[slot])

        @pl.when(turn == 0)
        def _():
            conv[...] = product

        @pl.when(turn > 0)
        def _():
            conv[...] += product

        return carry

    lax.fori_loop(0, 3, step, 0)

    column = lax.rem(lax.broadcasted_iota(jnp.int32, (positions, 1), 0), cols)
    before = pltpu.roll(conv[:, :channels], 1, 0)
    after = pltpu.roll(conv[:, 2 * channels :], positions - 1, 0)
    summed = (
        jnp.where(column == 0, 0.0, before)
        + conv[:, channels : 2 * channels]
        + jnp.where(column == cols - 1, 0.0, after)
    )
    rounded = (
        latent_ref[...].reshape(positions, channels).astype(jnp.float32) + summed
    ).astype(jnp.bfloat16)
    residual[...] = rounded
    wide = rounded.astype(jnp.float32)
    held[0] = (
        wide
        * lax.rsqrt(jnp.mean(wide * wide, axis=-1, keepdims=True) + 1e-06)
        * gain2_ref[...].reshape(1, channels)
    ).astype(jnp.bfloat16)

    for load in loads:
        load.wait()
    attend_ring(
        row_tiles,
        pieces,
        ring_left * 2 + frame,
        ring_right * 2 + frame,
        residual,
        wq,
        wk,
        wv,
        wo,
        out_ref,
        held,
        queries,
        highest,
        total,
        acc,
        send_sem,
        recv_sem,
    )

    for copy in cache_rows + onward:
        copy.wait_send()

    @pl.when(owned + 1 < row_tiles)
    def _():
        cache_rim.wait_send()

    @pl.when(jnp.logical_not(last))
    def _():
        rim_down.wait_send()

    @pl.when(jnp.logical_not(first))
    def _():
        rim_up.wait_send()


def whole_block(latent, cache, norm_gain, conv_kernel, attend_gain, weights, row_tiles, pieces=2):
    rows, cols, channels = latent.shape
    positions = rows * cols
    held_in_vmem = pl.BlockSpec(memory_space=pltpu.VMEM)
    return pl.pallas_call(
        functools.partial(block_kernel, row_tiles, pieces),
        out_shape=jax.ShapeDtypeStruct((positions, channels), jnp.bfloat16),
        in_specs=[pl.BlockSpec(memory_space=pltpu.HBM)] * 9,
        out_specs=held_in_vmem,
        scratch_shapes=ring_scratch(row_tiles, pieces, positions, channels)
        + [
            pltpu.VMEM((3, rows + 2, cols, channels), jnp.bfloat16),
            pltpu.VMEM((3, 3 * channels, 3 * channels), jnp.bfloat16),
            pltpu.VMEM((positions, 3 * channels), jnp.float32),
            pltpu.VMEM((positions, channels), jnp.bfloat16),
        ]
        + [pltpu.VMEM((channels, channels), jnp.bfloat16)] * 4
        + [
            pltpu.VMEM((rows, cols, channels), jnp.bfloat16),
            pltpu.VMEM((channels,), jnp.float32),
            pltpu.VMEM((channels,), jnp.float32),
            pltpu.SemaphoreType.DMA((3, 3, 3)),
            pltpu.SemaphoreType.DMA((8,)),
            pltpu.SemaphoreType.DMA((2 * rows + 5,)),
            pltpu.SemaphoreType.DMA((3, rows + 2)),
        ],
        compiler_params=pltpu.CompilerParams(
            collective_id=0, has_side_effects=True, vmem_limit_bytes=36 * 2**20
        ),
    )(
        latent,
        cache,
        norm_gain,
        conv_kernel,
        attend_gain,
        *weights,
    )


def body(
    video_latent, conv_cache, norm_gain, conv_kernel, attend_gain, w_query, w_key, w_value, w_output
):
    rows_local, cols_all, channels = video_latent.shape
    tiles = lax.axis_size("tile")
    row_tiles = min(16, tiles // 2)
    frames = tiles // row_tiles
    if frames == 2 and row_tiles > 4:
        result = whole_block(
            video_latent,
            conv_cache,
            norm_gain,
            conv_kernel,
            attend_gain,
            (w_query, w_key, w_value, w_output),
            row_tiles,
        )
        return result.reshape(video_latent.shape)
    position = lax.axis_index("tile")
    time_group = position % frames
    activated = jax.nn.silu(rms_scale(video_latent, norm_gain)).astype(jnp.bfloat16)
    frame_pair = jnp.stack([activated, conv_cache])
    before_one = from_behind(frame_pair, "tile", 1)
    before_two = from_behind(before_one, "tile", 1)
    frame_one = jnp.where(time_group >= 1, before_one[0], before_one[1])
    frame_two = jnp.where(time_group >= 2, before_two[0], before_two[1])
    stacked = jnp.stack([frame_two, frame_one, frame_pair[0]])
    rim_above = passed_along(stacked[:, -1:], "tile", frames)
    rim_below = passed_along(stacked[:, :1], "tile", -frames)
    stacked = jnp.concatenate([rim_above, stacked, rim_below], axis=1)
    padded = jnp.pad(stacked, ((0, 0), (0, 0), (1, 1), (0, 0)))
    summed = jnp.zeros((rows_local * cols_all, channels), jnp.float32)
    for time_tap in range(3):
        for row_tap in range(3):
            for col_tap in range(3):
                window = padded[
                    time_tap, row_tap : row_tap + rows_local, col_tap : col_tap + cols_all
                ]
                summed = summed + dot32(
                    window.reshape(-1, channels), conv_kernel[time_tap, row_tap, col_tap]
                )
    residual = (video_latent.astype(jnp.float32) + summed.reshape(video_latent.shape)).astype(
        jnp.bfloat16
    )
    normed = rms_scale(residual, attend_gain).astype(jnp.bfloat16)
    result = attend(
        normed.reshape(-1, channels),
        residual.reshape(-1, channels),
        (w_query, w_key, w_value, w_output),
        frames,
        row_tiles,
    )
    return result.reshape(video_latent.shape)


def solution(mesh):
    placed = (
        P(("groups", "tile"), None, None),
        P(("groups", "tile"), None, None),
        P(),
        P(),
        P(),
        P(),
        P(),
        P(),
        P(),
    )
    return jax.shard_map(
        body,
        mesh=mesh,
        in_specs=placed,
        out_specs=P(("groups", "tile"), None, None),
        check_vma=False,
    )
```

```python
import functools

import jax
import jax.numpy as jnp
from jax import lax
from jax.experimental import pallas as pl
from jax.experimental.pallas import tpu as pltpu
from jax.sharding import PartitionSpec as P


def from_behind(value, axis, steps):
    count = lax.axis_size(axis)
    pairs = [(source, (source + steps) % count) for source in range(count)]
    return lax.ppermute(value, axis, pairs)


def passed_along(block, axis, distance):
    devices = range(lax.axis_size(axis))
    route = [(i - distance, i) for i in devices if i - distance in devices]
    return lax.ppermute(block, axis, route)


def rms_scale(inputs, scale_gain):
    floats = inputs.astype(jnp.float32)
    return (
        floats * lax.rsqrt(jnp.mean(floats * floats, axis=-1, keepdims=True) + 1e-06) * scale_gain
    )


def dot32(a, b):
    return jnp.dot(a, b, preferred_element_type=jnp.float32)


def ring_tile(place, row_tiles):
    half = row_tiles // 2
    return jnp.where(place < half, 2 * place, 2 * (row_tiles - 1 - place) + 1)


MESH = pl.DeviceIdType.MESH


def place_of(tile, row_tiles):
    return jnp.where(lax.rem(tile, 2) == 0, lax.div(tile, 2), row_tiles - 1 - lax.div(tile, 2))


def ring_neighbours(tile, row_tiles):
    place = place_of(tile, row_tiles)
    right = ring_tile(lax.rem(place + 1, row_tiles), row_tiles)
    left = ring_tile(lax.rem(place + row_tiles - 1, row_tiles), row_tiles)
    return left, right


def attend_ring(
    row_tiles,
    pieces,
    left,
    right,
    residual_ref,
    wq_ref,
    wk_ref,
    wv_ref,
    wo_ref,
    out_ref,
    held,
    queries,
    highest,
    total,
    acc,
    send_sem,
    recv_sem,
):
    positions, channels = residual_ref.shape
    half = row_tiles // 2
    piece = positions // pieces
    scale = float(channels) ** (-0.5)

    def copy(way, step, part):
        if way == 0:
            source, target, peer = step - 1, step, right
        else:
            source, target, peer = (
                lax.rem(row_tiles - step + 1, row_tiles),
                row_tiles - step,
                left,
            )
        rows = pl.ds(pl.multiple_of(part * piece, piece), piece)
        return pltpu.make_async_remote_copy(
            src_ref=held.at[source, rows],
            dst_ref=held.at[target, rows],
            send_sem=send_sem.at[way, step, part],
            recv_sem=recv_sem.at[way, step, part],
            device_id={"tile": peer},
            device_id_type=pl.DeviceIdType.MESH,
        )

    def runs(way, step, part):
        last = (part < pieces // 2) if way == 0 else (part >= pieces // 2)
        return jnp.logical_or(step < half, jnp.logical_and(step == half, last))

    for part in range(pieces):
        for way in range(2):
            copy(way, 1, part).start()

    queries[...] = dot32(held[0], wq_ref[...]).astype(jnp.bfloat16)
    highest[...] = jnp.full(highest.shape, -1e30, jnp.float32)
    total[...] = jnp.zeros(total.shape, jnp.float32)
    acc[...] = jnp.zeros(acc.shape, jnp.float32)

    def absorb(slot, part):
        rows = pl.ds(pl.multiple_of(part * piece, piece), piece)
        block = held[slot, rows]
        keys = dot32(block, wk_ref[...]).astype(jnp.bfloat16)
        values = dot32(block, wv_ref[...]).astype(jnp.bfloat16)
        scores = (
            lax.dot_general(
                queries[...], keys, (((1,), (1,)), ((), ())), preferred_element_type=jnp.float32
            )
            * scale
        )
        before = highest[...]
        now = jnp.maximum(before, jnp.max(scores, axis=-1, keepdims=True))
        rescale = jnp.exp(before - now)
        weights = jnp.exp(scores - now)
        highest[...] = now
        total[...] = total[...] * rescale + jnp.sum(weights, axis=-1, keepdims=True)
        acc[...] = acc[...] * rescale + dot32(weights.astype(jnp.bfloat16), values)

    def own(part, carry):
        absorb(0, part)
        return carry

    lax.fori_loop(0, pieces, own, 0)

    def visit(index, carry):
        step = lax.div(index, pieces) + 1
        part = lax.rem(index, pieces)
        for way in range(2):

            @pl.when(runs(way, step, part))
            def _(way=way):
                copy(way, step, part).wait_recv()

            @pl.when(runs(way, step + 1, part))
            def _(way=way):
                copy(way, step + 1, part).start()

        def one(way, carry):
            absorb(jnp.where(way == 0, step, row_tiles - step), part)
            return carry

        lax.fori_loop(0, jnp.where(step == half, 1, 2), one, 0)
        return carry

    lax.fori_loop(0, half * pieces, visit, 0)

    attended = (acc[...] / total[...]).astype(jnp.bfloat16)
    out_ref[...] = (
        residual_ref[...].astype(jnp.float32) + dot32(attended, wo_ref[...])
    ).astype(jnp.bfloat16)

    def finish(index, carry):
        step = lax.div(index, pieces) + 1
        part = lax.rem(index, pieces)
        for way in range(2):

            @pl.when(runs(way, step, part))
            def _(way=way):
                copy(way, step, part).wait_send()

        return carry

    lax.fori_loop(0, half * pieces, finish, 0)


def attend_kernel(
    frames, row_tiles, pieces, normed_ref, residual_ref, wq, wk, wv, wo, out_ref, held, *scratch
):
    me = lax.axis_index("tile")
    frame = lax.rem(me, frames)
    left, right = ring_neighbours(lax.div(me, frames), row_tiles)
    left, right = left * frames + frame, right * frames + frame
    barrier = pltpu.get_barrier_semaphore()
    for neighbour in (left, right):
        pl.semaphore_signal(barrier, inc=1, device_id={"tile": neighbour}, device_id_type=MESH)
    held[0] = normed_ref[...]
    pl.semaphore_wait(barrier, 2)
    attend_ring(
        row_tiles, pieces, left, right, residual_ref, wq, wk, wv, wo, out_ref, held, *scratch
    )


def ring_scratch(row_tiles, pieces, positions, channels):
    half = row_tiles // 2
    return [
        pltpu.VMEM((row_tiles, positions, channels), jnp.bfloat16),
        pltpu.VMEM((positions, channels), jnp.bfloat16),
        pltpu.VMEM((positions, 1), jnp.float32),
        pltpu.VMEM((positions, 1), jnp.float32),
        pltpu.VMEM((positions, channels), jnp.float32),
        pltpu.SemaphoreType.DMA((2, half + 1, pieces)),
        pltpu.SemaphoreType.DMA((2, half + 1, pieces)),
    ]


def attend(normed, residual, weights, frames, row_tiles, pieces=2):
    positions, channels = normed.shape
    return pl.pallas_call(
        functools.partial(attend_kernel, frames, row_tiles, pieces),
        out_shape=jax.ShapeDtypeStruct((positions, channels), jnp.bfloat16),
        in_specs=[pl.BlockSpec(memory_space=pltpu.VMEM)] * 6,
        out_specs=pl.BlockSpec(memory_space=pltpu.VMEM),
        scratch_shapes=ring_scratch(row_tiles, pieces, positions, channels),
        compiler_params=pltpu.CompilerParams(
            collective_id=0, has_side_effects=True, vmem_limit_bytes=40 * 2**20
        ),
    )(normed, residual, *weights)


def block_kernel(
    row_tiles,
    pieces,
    latent_hbm,
    cache_ref,
    gain_hbm,
    kernel_ref,
    gain2_hbm,
    wq_hbm,
    wk_hbm,
    wv_hbm,
    wo_hbm,
    out_ref,
    held,
    queries,
    highest,
    total,
    acc,
    send_sem,
    recv_sem,
    stack,
    taps,
    conv,
    residual,
    wq,
    wk,
    wv,
    wo,
    latent_ref,
    gain_ref,
    gain2_ref,
    tap_sem,
    weight_sem,
    out_sem,
    row_sem,
):
    rows, cols, channels = latent_hbm.shape
    positions = rows * cols
    me = lax.axis_index("tile")
    frame = lax.rem(me, 2)
    tile = lax.div(me, 2)
    other = me + 1 - 2 * frame
    ring_left, ring_right = ring_neighbours(tile, row_tiles)

    def wrapped(by):
        return lax.rem(tile + by + row_tiles, row_tiles) * 2 + frame

    barrier = pltpu.get_barrier_semaphore()
    for partner in (wrapped(1), wrapped(-1), wrapped(2), wrapped(-2), other):
        pl.semaphore_signal(barrier, inc=1, device_id={"tile": partner}, device_id_type=MESH)

    early = [
        pltpu.make_async_copy(source, target, weight_sem.at[5 + number])
        for number, (source, target) in enumerate(
            ((latent_hbm, latent_ref), (gain_hbm, gain_ref), (gain2_hbm, gain2_ref))
        )
    ]
    for load in early:
        load.start()

    def tap_copy(t, i, j):
        return pltpu.make_async_copy(
            kernel_ref.at[t, i, j],
            taps.at[t, i * channels : (i + 1) * channels, j * channels : (j + 1) * channels],
            tap_sem.at[t, i, j],
        )

    every = [(i, j) for i in range(3) for j in range(3)]
    for t in (2, 0, 1):
        for i, j in every:
            tap_copy(t, i, j).start()
    loads = [
        pltpu.make_async_copy(source, target, weight_sem.at[number])
        for number, (source, target) in enumerate(
            ((wq_hbm, wq), (wk_hbm, wk), (wv_hbm, wv), (wo_hbm, wo))
        )
    ]
    for load in loads:
        load.start()

    first, last = tile == 0, tile == row_tiles - 1
    owned = lax.rem(tile + 1, row_tiles)

    def send(source, slot, row, number, device):
        return pltpu.make_async_remote_copy(
            src_ref=source,
            dst_ref=stack.at[slot, row],
            send_sem=out_sem.at[number],
            recv_sem=row_sem.at[slot, row],
            device_id={"tile": device},
            device_id_type=MESH,
        )

    cache_rows = [send(cache_ref.at[j], 0, 1 + j, j, wrapped(1)) for j in range(rows)]
    cache_rim = send(cache_ref.at[rows - 1], 0, 0, rows, wrapped(2))
    rim_down = send(stack.at[2, rows], 2, 0, rows + 1, wrapped(1))
    rim_up = send(stack.at[2, 1], 2, rows + 1, rows + 2, wrapped(-1))
    shared = 2 - 2 * frame
    onward = [send(stack.at[shared, j], 1, j, rows + 3 + j, other) for j in range(rows + 2)]

    own_rim = pltpu.make_async_copy(cache_ref.at[0], stack.at[0, rows + 1], weight_sem.at[4])
    pl.semaphore_wait(barrier, 5)
    cache_rows[0].start()

    @pl.when(owned + 1 < row_tiles)
    def _():
        cache_rim.start()

    for load in early:
        load.wait()
    floats = latent_ref[...].astype(jnp.float32)
    scaled = (
        floats
        * lax.rsqrt(jnp.mean(floats * floats, axis=-1, keepdims=True) + 1e-06)
        * gain_ref[...].reshape(1, 1, channels)
    )
    stack[2, 1 : rows + 1] = (scaled / (1.0 + jnp.exp(-scaled))).astype(jnp.bfloat16)

    @pl.when(jnp.logical_not(last))
    def _():
        rim_down.start()

    @pl.when(jnp.logical_not(first))
    def _():
        rim_up.start()

    @pl.when(frame == 0)
    def _():
        for j in range(1, rows + 1):
            onward[j].start()

    for copy in cache_rows[1:]:
        copy.start()

    nothing = jnp.zeros((cols, channels), jnp.bfloat16)

    @pl.when(first)
    def _():
        stack[0, 0] = nothing
        stack[2, 0] = nothing

    @pl.when(last)
    def _():
        stack[0, rows + 1] = nothing
        stack[2, rows + 1] = nothing

    @pl.when(jnp.logical_not(last))
    def _():
        own_rim.start()
        own_rim.wait()

    def arrived(slot, row):
        send(stack.at[slot, row], slot, row, 0, other).wait_recv()

    def cached_in():
        for j in range(1, rows + 1):
            arrived(0, j)
            yield j

        @pl.when(jnp.logical_not(first))
        def _():
            arrived(0, 0)

        yield 0

    def step(turn, carry):
        slot = jnp.where(turn == 0, 2, jnp.where(turn == 1, frame, 1 - frame))

        @pl.when(turn == 0)
        def _():
            @pl.when(jnp.logical_not(first))
            def _():
                arrived(2, 0)

            @pl.when(jnp.logical_not(last))
            def _():
                arrived(2, rows + 1)

            @pl.when(frame == 0)
            def _():
                onward[0].start()
                onward[rows + 1].start()

            @pl.when(frame == 1)
            def _():
                onward[rows + 1].start()

        @pl.when(jnp.logical_and(turn > 0, slot == 1))
        def _():
            for j in range(rows + 2):
                arrived(1, j)

        @pl.when(jnp.logical_and(turn > 0, jnp.logical_and(slot == 0, frame == 0)))
        def _():
            for j in cached_in():
                pass

        @pl.when(jnp.logical_and(turn > 0, jnp.logical_and(slot == 0, frame == 1)))
        def _():
            for j in cached_in():
                onward[j].start()

        for i, j in every:
            pltpu.make_async_copy(
                kernel_ref.at[slot, i, j],
                taps.at[
                    slot, i * channels : (i + 1) * channels, j * channels : (j + 1) * channels
                ],
                tap_sem.at[slot, i, j],
            ).wait()

        window = jnp.concatenate(
            [stack[slot, i : i + rows].reshape(positions, channels) for i in range(3)], axis=-1
        )
        product = dot32(window, taps[slot])

        @pl.when(turn == 0)
        def _():
            conv[...] = product

        @pl.when(turn > 0)
        def _():
            conv[...] += product

        return carry

    lax.fori_loop(0, 3, step, 0)

    column = lax.rem(lax.broadcasted_iota(jnp.int32, (positions, 1), 0), cols)
    before = pltpu.roll(conv[:, :channels], 1, 0)
    after = pltpu.roll(conv[:, 2 * channels :], positions - 1, 0)
    summed = (
        jnp.where(column == 0, 0.0, before)
        + conv[:, channels : 2 * channels]
        + jnp.where(column == cols - 1, 0.0, after)
    )
    rounded = (
        latent_ref[...].reshape(positions, channels).astype(jnp.float32) + summed
    ).astype(jnp.bfloat16)
    residual[...] = rounded
    wide = rounded.astype(jnp.float32)
    held[0] = (
        wide
        * lax.rsqrt(jnp.mean(wide * wide, axis=-1, keepdims=True) + 1e-06)
        * gain2_ref[...].reshape(1, channels)
    ).astype(jnp.bfloat16)

    for load in loads:
        load.wait()
    attend_ring(
        row_tiles,
        pieces,
        ring_left * 2 + frame,
        ring_right * 2 + frame,
        residual,
        wq,
        wk,
        wv,
        wo,
        out_ref,
        held,
        queries,
        highest,
        total,
        acc,
        send_sem,
        recv_sem,
    )

    for copy in cache_rows + onward:
        copy.wait_send()

    @pl.when(owned + 1 < row_tiles)
    def _():
        cache_rim.wait_send()

    @pl.when(jnp.logical_not(last))
    def _():
        rim_down.wait_send()

    @pl.when(jnp.logical_not(first))
    def _():
        rim_up.wait_send()


def whole_block(latent, cache, norm_gain, conv_kernel, attend_gain, weights, row_tiles, pieces=2):
    rows, cols, channels = latent.shape
    positions = rows * cols
    held_in_vmem = pl.BlockSpec(memory_space=pltpu.VMEM)
    return pl.pallas_call(
        functools.partial(block_kernel, row_tiles, pieces),
        out_shape=jax.ShapeDtypeStruct((positions, channels), jnp.bfloat16),
        in_specs=[pl.BlockSpec(memory_space=pltpu.HBM)] * 9,
        out_specs=held_in_vmem,
        scratch_shapes=ring_scratch(row_tiles, pieces, positions, channels)
        + [
            pltpu.VMEM((3, rows + 2, cols, channels), jnp.bfloat16),
            pltpu.VMEM((3, 3 * channels, 3 * channels), jnp.bfloat16),
            pltpu.VMEM((positions, 3 * channels), jnp.float32),
            pltpu.VMEM((positions, channels), jnp.bfloat16),
        ]
        + [pltpu.VMEM((channels, channels), jnp.bfloat16)] * 4
        + [
            pltpu.VMEM((rows, cols, channels), jnp.bfloat16),
            pltpu.VMEM((channels,), jnp.float32),
            pltpu.VMEM((channels,), jnp.float32),
            pltpu.SemaphoreType.DMA((3, 3, 3)),
            pltpu.SemaphoreType.DMA((8,)),
            pltpu.SemaphoreType.DMA((2 * rows + 5,)),
            pltpu.SemaphoreType.DMA((3, rows + 2)),
        ],
        compiler_params=pltpu.CompilerParams(
            collective_id=0, has_side_effects=True, vmem_limit_bytes=58 * 2**20
        ),
    )(
        latent,
        cache,
        norm_gain,
        conv_kernel,
        attend_gain,
        *weights,
    )


def body(
    video_latent, conv_cache, norm_gain, conv_kernel, attend_gain, w_query, w_key, w_value, w_output
):
    rows_local, cols_all, channels = video_latent.shape
    tiles = lax.axis_size("tile")
    row_tiles = min(16, tiles // 2)
    frames = tiles // row_tiles
    if frames == 2 and row_tiles > 4:
        result = whole_block(
            video_latent,
            conv_cache,
            norm_gain,
            conv_kernel,
            attend_gain,
            (w_query, w_key, w_value, w_output),
            row_tiles,
        )
        return result.reshape(video_latent.shape)
    position = lax.axis_index("tile")
    time_group = position % frames
    activated = jax.nn.silu(rms_scale(video_latent, norm_gain)).astype(jnp.bfloat16)
    frame_pair = jnp.stack([activated, conv_cache])
    before_one = from_behind(frame_pair, "tile", 1)
    before_two = from_behind(before_one, "tile", 1)
    frame_one = jnp.where(time_group >= 1, before_one[0], before_one[1])
    frame_two = jnp.where(time_group >= 2, before_two[0], before_two[1])
    stacked = jnp.stack([frame_two, frame_one, frame_pair[0]])
    rim_above = passed_along(stacked[:, -1:], "tile", frames)
    rim_below = passed_along(stacked[:, :1], "tile", -frames)
    stacked = jnp.concatenate([rim_above, stacked, rim_below], axis=1)
    padded = jnp.pad(stacked, ((0, 0), (0, 0), (1, 1), (0, 0)))
    summed = jnp.zeros((rows_local * cols_all, channels), jnp.float32)
    for time_tap in range(3):
        for row_tap in range(3):
            for col_tap in range(3):
                window = padded[
                    time_tap, row_tap : row_tap + rows_local, col_tap : col_tap + cols_all
                ]
                summed = summed + dot32(
                    window.reshape(-1, channels), conv_kernel[time_tap, row_tap, col_tap]
                )
    residual = (video_latent.astype(jnp.float32) + summed.reshape(video_latent.shape)).astype(
        jnp.bfloat16
    )
    normed = rms_scale(residual, attend_gain).astype(jnp.bfloat16)
    result = attend(
        normed.reshape(-1, channels),
        residual.reshape(-1, channels),
        (w_query, w_key, w_value, w_output),
        frames,
        row_tiles,
    )
    return result.reshape(video_latent.shape)


def solution(mesh):
    placed = (
        P(("groups", "tile"), None, None),
        P(("groups", "tile"), None, None),
        P(),
        P(),
        P(),
        P(),
        P(),
        P(),
        P(),
    )
    return jax.shard_map(
        body,
        mesh=mesh,
        in_specs=placed,
        out_specs=P(("groups", "tile"), None, None),
        check_vma=False,
    )
```

```python
import functools

import jax
import jax.numpy as jnp
from jax import lax
from jax.experimental import pallas as pl
from jax.experimental.pallas import tpu as pltpu
from jax.sharding import PartitionSpec as P


def from_behind(value, axis, steps):
    count = lax.axis_size(axis)
    pairs = [(source, (source + steps) % count) for source in range(count)]
    return lax.ppermute(value, axis, pairs)


def passed_along(block, axis, distance):
    devices = range(lax.axis_size(axis))
    route = [(i - distance, i) for i in devices if i - distance in devices]
    return lax.ppermute(block, axis, route)


def rms_scale(inputs, scale_gain):
    floats = inputs.astype(jnp.float32)
    return (
        floats * lax.rsqrt(jnp.mean(floats * floats, axis=-1, keepdims=True) + 1e-06) * scale_gain
    )


def dot32(a, b):
    return jnp.dot(a, b, preferred_element_type=jnp.float32)


def ring_tile(place, row_tiles):
    half = row_tiles // 2
    return jnp.where(place < half, 2 * place, 2 * (row_tiles - 1 - place) + 1)


MESH = pl.DeviceIdType.MESH


def place_of(tile, row_tiles):
    return jnp.where(lax.rem(tile, 2) == 0, lax.div(tile, 2), row_tiles - 1 - lax.div(tile, 2))


def ring_neighbours(tile, row_tiles):
    place = place_of(tile, row_tiles)
    right = ring_tile(lax.rem(place + 1, row_tiles), row_tiles)
    left = ring_tile(lax.rem(place + row_tiles - 1, row_tiles), row_tiles)
    return left, right


def attend_ring(
    row_tiles,
    pieces,
    left,
    right,
    residual_ref,
    wq_ref,
    wk_ref,
    wv_ref,
    wo_ref,
    out_ref,
    held,
    queries,
    highest,
    total,
    acc,
    send_sem,
    recv_sem,
):
    positions, channels = residual_ref.shape
    half = row_tiles // 2
    piece = positions // pieces
    scale = float(channels) ** (-0.5)

    def copy(way, step, part):
        if way == 0:
            source, target, peer = step - 1, step, right
        else:
            source, target, peer = (
                lax.rem(row_tiles - step + 1, row_tiles),
                row_tiles - step,
                left,
            )
        rows = pl.ds(pl.multiple_of(part * piece, piece), piece)
        return pltpu.make_async_remote_copy(
            src_ref=held.at[source, rows],
            dst_ref=held.at[target, rows],
            send_sem=send_sem.at[way, step, part],
            recv_sem=recv_sem.at[way, step, part],
            device_id={"tile": peer},
            device_id_type=pl.DeviceIdType.MESH,
        )

    def runs(way, step, part):
        last = (part < pieces // 2) if way == 0 else (part >= pieces // 2)
        return jnp.logical_or(step < half, jnp.logical_and(step == half, last))

    for part in range(pieces):
        for way in range(2):
            copy(way, 1, part).start()

    queries[...] = dot32(held[0], wq_ref[...]).astype(jnp.bfloat16)
    highest[...] = jnp.full(highest.shape, -1e30, jnp.float32)
    total[...] = jnp.zeros(total.shape, jnp.float32)
    acc[...] = jnp.zeros(acc.shape, jnp.float32)

    def absorb(slot, part):
        rows = pl.ds(pl.multiple_of(part * piece, piece), piece)
        block = held[slot, rows]
        keys = dot32(block, wk_ref[...]).astype(jnp.bfloat16)
        values = dot32(block, wv_ref[...]).astype(jnp.bfloat16)
        scores = (
            lax.dot_general(
                queries[...], keys, (((1,), (1,)), ((), ())), preferred_element_type=jnp.float32
            )
            * scale
        )
        before = highest[...]
        now = jnp.maximum(before, jnp.max(scores, axis=-1, keepdims=True))
        rescale = jnp.exp(before - now)
        weights = jnp.exp(scores - now)
        highest[...] = now
        total[...] = total[...] * rescale + jnp.sum(weights, axis=-1, keepdims=True)
        acc[...] = acc[...] * rescale + dot32(weights.astype(jnp.bfloat16), values)

    def own(part, carry):
        absorb(0, part)
        return carry

    lax.fori_loop(0, pieces, own, 0)

    def visit(index, carry):
        step = lax.div(index, pieces) + 1
        part = lax.rem(index, pieces)
        for way in range(2):

            @pl.when(runs(way, step, part))
            def _(way=way):
                copy(way, step, part).wait_recv()

            @pl.when(runs(way, step + 1, part))
            def _(way=way):
                copy(way, step + 1, part).start()

        def one(way, carry):
            absorb(jnp.where(way == 0, step, row_tiles - step), part)
            return carry

        lax.fori_loop(0, jnp.where(step == half, 1, 2), one, 0)
        return carry

    lax.fori_loop(0, half * pieces, visit, 0)

    attended = (acc[...] / total[...]).astype(jnp.bfloat16)
    out_ref[...] = (
        residual_ref[...].astype(jnp.float32) + dot32(attended, wo_ref[...])
    ).astype(jnp.bfloat16)

    def finish(index, carry):
        step = lax.div(index, pieces) + 1
        part = lax.rem(index, pieces)
        for way in range(2):

            @pl.when(runs(way, step, part))
            def _(way=way):
                copy(way, step, part).wait_send()

        return carry

    lax.fori_loop(0, half * pieces, finish, 0)


def attend_kernel(
    frames, row_tiles, pieces, normed_ref, residual_ref, wq, wk, wv, wo, out_ref, held, *scratch
):
    me = lax.axis_index("tile")
    frame = lax.rem(me, frames)
    left, right = ring_neighbours(lax.div(me, frames), row_tiles)
    left, right = left * frames + frame, right * frames + frame
    barrier = pltpu.get_barrier_semaphore()
    for neighbour in (left, right):
        pl.semaphore_signal(barrier, inc=1, device_id={"tile": neighbour}, device_id_type=MESH)
    held[0] = normed_ref[...]
    pl.semaphore_wait(barrier, 2)
    attend_ring(
        row_tiles, pieces, left, right, residual_ref, wq, wk, wv, wo, out_ref, held, *scratch
    )


def ring_scratch(row_tiles, pieces, positions, channels):
    half = row_tiles // 2
    return [
        pltpu.VMEM((row_tiles, positions, channels), jnp.bfloat16),
        pltpu.VMEM((positions, channels), jnp.bfloat16),
        pltpu.VMEM((positions, 1), jnp.float32),
        pltpu.VMEM((positions, 1), jnp.float32),
        pltpu.VMEM((positions, channels), jnp.float32),
        pltpu.SemaphoreType.DMA((2, half + 1, pieces)),
        pltpu.SemaphoreType.DMA((2, half + 1, pieces)),
    ]


def attend(normed, residual, weights, frames, row_tiles, pieces=2):
    positions, channels = normed.shape
    return pl.pallas_call(
        functools.partial(attend_kernel, frames, row_tiles, pieces),
        out_shape=jax.ShapeDtypeStruct((positions, channels), jnp.bfloat16),
        in_specs=[pl.BlockSpec(memory_space=pltpu.VMEM)] * 6,
        out_specs=pl.BlockSpec(memory_space=pltpu.VMEM),
        scratch_shapes=ring_scratch(row_tiles, pieces, positions, channels),
        compiler_params=pltpu.CompilerParams(
            collective_id=0, has_side_effects=True, vmem_limit_bytes=40 * 2**20
        ),
    )(normed, residual, *weights)


def block_kernel(
    row_tiles,
    pieces,
    latent_hbm,
    cache_ref,
    gain_hbm,
    kernel_ref,
    gain2_hbm,
    wq_hbm,
    wk_hbm,
    wv_hbm,
    wo_hbm,
    out_ref,
    held,
    queries,
    highest,
    total,
    acc,
    send_sem,
    recv_sem,
    stack,
    taps,
    conv,
    residual,
    wq,
    wk,
    wv,
    wo,
    latent_ref,
    gain_ref,
    gain2_ref,
    tap_sem,
    weight_sem,
    out_sem,
    row_sem,
):
    rows, cols, channels = latent_hbm.shape
    positions = rows * cols
    me = lax.axis_index("tile")
    frame = lax.rem(me, 2)
    tile = lax.div(me, 2)
    other = me + 1 - 2 * frame
    ring_left, ring_right = ring_neighbours(tile, row_tiles)

    def wrapped(by):
        return lax.rem(tile + by + row_tiles, row_tiles) * 2 + frame

    barrier = pltpu.get_barrier_semaphore()
    for partner in (wrapped(1), wrapped(-1), wrapped(2), wrapped(-2), other):
        pl.semaphore_signal(barrier, inc=1, device_id={"tile": partner}, device_id_type=MESH)

    early = [
        pltpu.make_async_copy(source, target, weight_sem.at[5 + number])
        for number, (source, target) in enumerate(
            ((latent_hbm, latent_ref), (gain_hbm, gain_ref), (gain2_hbm, gain2_ref))
        )
    ]
    for load in early:
        load.start()

    def tap_copy(t, i, j):
        return pltpu.make_async_copy(
            kernel_ref.at[t, i, j],
            taps.at[t, i * channels : (i + 1) * channels, j * channels : (j + 1) * channels],
            tap_sem.at[t, i, j],
        )

    every = [(i, j) for i in range(3) for j in range(3)]
    for turn in range(3):
        for i, j in every:
            tap_copy(jnp.where(frame == 0, 2 - turn, turn), i, j).start()
    loads = [
        pltpu.make_async_copy(source, target, weight_sem.at[number])
        for number, (source, target) in enumerate(
            ((wq_hbm, wq), (wk_hbm, wk), (wv_hbm, wv), (wo_hbm, wo))
        )
    ]
    for load in loads:
        load.start()

    first, last = tile == 0, tile == row_tiles - 1
    owned = lax.rem(tile + 1, row_tiles)

    def send(source, slot, row, number, device):
        return pltpu.make_async_remote_copy(
            src_ref=source,
            dst_ref=stack.at[slot, row],
            send_sem=out_sem.at[number],
            recv_sem=row_sem.at[slot, row],
            device_id={"tile": device},
            device_id_type=MESH,
        )

    cache_rows = [send(cache_ref.at[j], 0, 1 + j, j, wrapped(1)) for j in range(rows)]
    cache_rim = send(cache_ref.at[rows - 1], 0, 0, rows, wrapped(2))
    rim_down = send(stack.at[2, rows], 2, 0, rows + 1, wrapped(1))
    rim_up = send(stack.at[2, 1], 2, rows + 1, rows + 2, wrapped(-1))
    shared = 2 - 2 * frame
    onward = [send(stack.at[shared, j], 1, j, rows + 3 + j, other) for j in range(rows + 2)]

    own_rim = pltpu.make_async_copy(cache_ref.at[0], stack.at[0, rows + 1], weight_sem.at[4])
    pl.semaphore_wait(barrier, 5)

    @pl.when(frame == 1)
    def _():
        for copy in cache_rows:
            copy.start()

    @pl.when(owned + 1 < row_tiles)
    def _():
        cache_rim.start()

    for load in early:
        load.wait()
    floats = latent_ref[...].astype(jnp.float32)
    scaled = (
        floats
        * lax.rsqrt(jnp.mean(floats * floats, axis=-1, keepdims=True) + 1e-06)
        * gain_ref[...].reshape(1, 1, channels)
    )
    stack[2, 1 : rows + 1] = (scaled / (1.0 + jnp.exp(-scaled))).astype(jnp.bfloat16)

    @pl.when(jnp.logical_not(last))
    def _():
        rim_down.start()

    @pl.when(jnp.logical_not(first))
    def _():
        rim_up.start()

    @pl.when(frame == 0)
    def _():
        for j in range(1, rows + 1):
            onward[j].start()

    @pl.when(frame == 0)
    def _():
        for copy in cache_rows:
            copy.start()

    nothing = jnp.zeros((cols, channels), jnp.bfloat16)

    @pl.when(first)
    def _():
        stack[0, 0] = nothing
        stack[2, 0] = nothing

    @pl.when(last)
    def _():
        stack[0, rows + 1] = nothing
        stack[2, rows + 1] = nothing

    @pl.when(jnp.logical_not(last))
    def _():
        own_rim.start()
        own_rim.wait()

    def arrived(slot, row):
        send(stack.at[slot, row], slot, row, 0, other).wait_recv()

    def cached_in():
        for j in range(1, rows + 1):
            arrived(0, j)
            yield j

        @pl.when(jnp.logical_not(first))
        def _():
            arrived(0, 0)

        yield 0

    def step(turn, carry):
        slot = jnp.where(frame == 0, 2 - turn, turn)

        @pl.when(slot == 2)
        def _():
            @pl.when(jnp.logical_not(first))
            def _():
                arrived(2, 0)

            @pl.when(jnp.logical_not(last))
            def _():
                arrived(2, rows + 1)

            @pl.when(frame == 0)
            def _():
                onward[0].start()
                onward[rows + 1].start()

        @pl.when(slot == 1)
        def _():
            for j in range(rows + 2):
                arrived(1, j)

        @pl.when(jnp.logical_and(slot == 0, frame == 0))
        def _():
            for j in cached_in():
                pass

        @pl.when(jnp.logical_and(slot == 0, frame == 1))
        def _():
            onward[rows + 1].start()
            for j in cached_in():
                onward[j].start()

        for i, j in every:
            pltpu.make_async_copy(
                kernel_ref.at[slot, i, j],
                taps.at[
                    slot, i * channels : (i + 1) * channels, j * channels : (j + 1) * channels
                ],
                tap_sem.at[slot, i, j],
            ).wait()

        window = jnp.concatenate(
            [stack[slot, i : i + rows].reshape(positions, channels) for i in range(3)], axis=-1
        )
        product = dot32(window, taps[slot])

        @pl.when(turn == 0)
        def _():
            conv[...] = product

        @pl.when(turn > 0)
        def _():
            conv[...] += product

        return carry

    lax.fori_loop(0, 3, step, 0)

    column = lax.rem(lax.broadcasted_iota(jnp.int32, (positions, 1), 0), cols)
    before = pltpu.roll(conv[:, :channels], 1, 0)
    after = pltpu.roll(conv[:, 2 * channels :], positions - 1, 0)
    summed = (
        jnp.where(column == 0, 0.0, before)
        + conv[:, channels : 2 * channels]
        + jnp.where(column == cols - 1, 0.0, after)
    )
    rounded = (
        latent_ref[...].reshape(positions, channels).astype(jnp.float32) + summed
    ).astype(jnp.bfloat16)
    residual[...] = rounded
    wide = rounded.astype(jnp.float32)
    held[0] = (
        wide
        * lax.rsqrt(jnp.mean(wide * wide, axis=-1, keepdims=True) + 1e-06)
        * gain2_ref[...].reshape(1, channels)
    ).astype(jnp.bfloat16)

    for load in loads:
        load.wait()
    attend_ring(
        row_tiles,
        pieces,
        ring_left * 2 + frame,
        ring_right * 2 + frame,
        residual,
        wq,
        wk,
        wv,
        wo,
        out_ref,
        held,
        queries,
        highest,
        total,
        acc,
        send_sem,
        recv_sem,
    )

    for copy in cache_rows + onward:
        copy.wait_send()

    @pl.when(owned + 1 < row_tiles)
    def _():
        cache_rim.wait_send()

    @pl.when(jnp.logical_not(last))
    def _():
        rim_down.wait_send()

    @pl.when(jnp.logical_not(first))
    def _():
        rim_up.wait_send()


def whole_block(latent, cache, norm_gain, conv_kernel, attend_gain, weights, row_tiles, pieces=2):
    rows, cols, channels = latent.shape
    positions = rows * cols
    held_in_vmem = pl.BlockSpec(memory_space=pltpu.VMEM)
    return pl.pallas_call(
        functools.partial(block_kernel, row_tiles, pieces),
        out_shape=jax.ShapeDtypeStruct((positions, channels), jnp.bfloat16),
        in_specs=[pl.BlockSpec(memory_space=pltpu.HBM)] * 9,
        out_specs=held_in_vmem,
        scratch_shapes=ring_scratch(row_tiles, pieces, positions, channels)
        + [
            pltpu.VMEM((3, rows + 2, cols, channels), jnp.bfloat16),
            pltpu.VMEM((3, 3 * channels, 3 * channels), jnp.bfloat16),
            pltpu.VMEM((positions, 3 * channels), jnp.float32),
            pltpu.VMEM((positions, channels), jnp.bfloat16),
        ]
        + [pltpu.VMEM((channels, channels), jnp.bfloat16)] * 4
        + [
            pltpu.VMEM((rows, cols, channels), jnp.bfloat16),
            pltpu.VMEM((channels,), jnp.float32),
            pltpu.VMEM((channels,), jnp.float32),
            pltpu.SemaphoreType.DMA((3, 3, 3)),
            pltpu.SemaphoreType.DMA((8,)),
            pltpu.SemaphoreType.DMA((2 * rows + 5,)),
            pltpu.SemaphoreType.DMA((3, rows + 2)),
        ],
        compiler_params=pltpu.CompilerParams(
            collective_id=0, has_side_effects=True, vmem_limit_bytes=58 * 2**20
        ),
    )(
        latent,
        cache,
        norm_gain,
        conv_kernel,
        attend_gain,
        *weights,
    )


def body(
    video_latent, conv_cache, norm_gain, conv_kernel, attend_gain, w_query, w_key, w_value, w_output
):
    rows_local, cols_all, channels = video_latent.shape
    tiles = lax.axis_size("tile")
    row_tiles = min(16, tiles // 2)
    frames = tiles // row_tiles
    if frames == 2 and row_tiles > 4:
        result = whole_block(
            video_latent,
            conv_cache,
            norm_gain,
            conv_kernel,
            attend_gain,
            (w_query, w_key, w_value, w_output),
            row_tiles,
        )
        return result.reshape(video_latent.shape)
    position = lax.axis_index("tile")
    time_group = position % frames
    activated = jax.nn.silu(rms_scale(video_latent, norm_gain)).astype(jnp.bfloat16)
    frame_pair = jnp.stack([activated, conv_cache])
    before_one = from_behind(frame_pair, "tile", 1)
    before_two = from_behind(before_one, "tile", 1)
    frame_one = jnp.where(time_group >= 1, before_one[0], before_one[1])
    frame_two = jnp.where(time_group >= 2, before_two[0], before_two[1])
    stacked = jnp.stack([frame_two, frame_one, frame_pair[0]])
    rim_above = passed_along(stacked[:, -1:], "tile", frames)
    rim_below = passed_along(stacked[:, :1], "tile", -frames)
    stacked = jnp.concatenate([rim_above, stacked, rim_below], axis=1)
    padded = jnp.pad(stacked, ((0, 0), (0, 0), (1, 1), (0, 0)))
    summed = jnp.zeros((rows_local * cols_all, channels), jnp.float32)
    for time_tap in range(3):
        for row_tap in range(3):
            for col_tap in range(3):
                window = padded[
                    time_tap, row_tap : row_tap + rows_local, col_tap : col_tap + cols_all
                ]
                summed = summed + dot32(
                    window.reshape(-1, channels), conv_kernel[time_tap, row_tap, col_tap]
                )
    residual = (video_latent.astype(jnp.float32) + summed.reshape(video_latent.shape)).astype(
        jnp.bfloat16
    )
    normed = rms_scale(residual, attend_gain).astype(jnp.bfloat16)
    result = attend(
        normed.reshape(-1, channels),
        residual.reshape(-1, channels),
        (w_query, w_key, w_value, w_output),
        frames,
        row_tiles,
    )
    return result.reshape(video_latent.shape)


def solution(mesh):
    placed = (
        P(("groups", "tile"), None, None),
        P(("groups", "tile"), None, None),
        P(),
        P(),
        P(),
        P(),
        P(),
        P(),
        P(),
    )
    return jax.shard_map(
        body,
        mesh=mesh,
        in_specs=placed,
        out_specs=P(("groups", "tile"), None, None),
        check_vma=False,
    )
```
